256 devices in a mesh: gx: 8 (over x, core), gy: 32 (over y, z).
Axes of the slice: x: 4, y: 4, z: 8, core: 2. Of those that a mesh axis runs over, the one named last changes fastest.
Arguments:
- prompt: bfloat16 [512, 8192], P('gx'), may hold values from -6 to 6
- dec_in: bfloat16 [2, 256, 8192], P(None, 'gy', 'gx'), may hold values from -6 to 6
- gate_codes: bfloat16 [8192, 53248], P('gx', 'gy'), may hold values from -127 to 127, as said below
- gate_scale: float32 [64, 53248], P('gx', 'gy'), may hold values from 5e-05 to 0.0005
- up_codes: bfloat16 [8192, 53248], P('gx', 'gy'), may hold values from -127 to 127, as said below
- up_scale: float32 [64, 53248], P('gx', 'gy'), may hold values from 5e-05 to 0.0005
- down_codes: bfloat16 [53248, 8192], P('gy', 'gx'), may hold values from -127 to 127, as said below
- down_scale: float32 [53248, 64], P('gy', 'gx'), may hold values from 2.5e-05 to 0.00025
Outputs:
- prompt_out: bfloat16 [512, 8192], P('gy', 'gx')
- dec_out: bfloat16 [2, 256, 8192], P(None, 'gy', 'gx')
The draws below stay inside these ranges and needn't reach their ends.
Inputs may be any that keep to these rules, and one draw needn't show every extreme that they name: `gate_codes`: whole numbers. `up_codes`: whole numbers. `down_codes`: whole numbers.
All inputs are finite; a program needn't handle non-finite values.
Results may differ from the reference program's by a relative error of at most 0.034.
Values may be sent and summed in bfloat16 or wider, within the bound.
A program may use at most 192 MiB of HBM per device.

```python
import math
import jax
import jax.numpy as jnp
from jax import lax

D = 8192
FF = 53248
PRE_TOK = 512
DEC_ROWS = 256
DEC_STEPS = 2
N_GX = 8
N_GY = 32


def draw_gate_codes(key, part):
    key = jax.random.fold_in(key, 11)
    return jax.random.randint(key, (D, FF), -127, 128).astype(jnp.float32).astype(jnp.bfloat16)


def draw_up_codes(key, part):
    key = jax.random.fold_in(key, 23)
    return jax.random.randint(key, (D, FF), -127, 128).astype(jnp.float32).astype(jnp.bfloat16)


def draw_down_codes(key, part):
    key = jax.random.fold_in(key, 37)
    return jax.random.randint(key, (FF, D), -127, 128).astype(jnp.float32).astype(jnp.bfloat16)


def block_scale(key, shape, pieces, low, top_value):
    gain, own = 1.0, jax.random.fold_in(key, 6)
    for axis_at, blocks in pieces:
        draws = jnp.exp(jax.random.uniform(jax.random.fold_in(own, axis_at), (blocks,), jnp.float32, low / len(pieces), top_value / len(pieces)))
        gain = gain * jnp.repeat(draws, shape[axis_at] // blocks).reshape([-1 if axis == axis_at else 1 for axis in range(len(shape))])
    return gain


def bell_draw(own_key, shape, deviation, bound, split=(), kind=jnp.bfloat16):
    array = deviation * jax.random.normal(own_key, shape, jnp.float32)
    if split:
        array = array * block_scale(own_key, shape, split, -0.22, 0.18)
    return jnp.clip(array, -bound, bound).astype(kind)


def setup_inputs(seed: int = 0) -> dict:
    streams_of = jax.random.split(jax.random.key(seed), 9)
    prompt = bell_draw(streams_of[0], (PRE_TOK, D), 1.0, 6.0, ((0, 8),))
    dec_in = bell_draw(streams_of[1], (DEC_STEPS, DEC_ROWS, D), 1.0, 6.0, ((1, 32), (2, 8)))
    gate_codes = draw_gate_codes(jax.random.fold_in(streams_of[8], 71), 0)
    gate_scale = jnp.clip(jnp.exp(math.log(0.0005) - 2.3025852 * jax.random.uniform(streams_of[3], (D // 128, FF), jnp.float32) ** block_scale(streams_of[3], (D // 128, FF), ((0, 8), (1, 32)), -0.2, 0.2)), 4.999999873689376e-05, 0.0005)
    up_codes = draw_up_codes(jax.random.fold_in(streams_of[8], 71), 0)
    up_scale = jnp.clip(jnp.exp(math.log(0.0005) - 2.3025852 * jax.random.uniform(streams_of[5], (D // 128, FF), jnp.float32) ** block_scale(streams_of[5], (D // 128, FF), ((0, 8), (1, 32)), -0.2, 0.2)), 4.999999873689376e-05, 0.0005)
    down_codes = draw_down_codes(jax.random.fold_in(streams_of[8], 71), 0)
    down_scale = jnp.clip(jnp.exp(math.log(0.00025) - 2.3025852 * jax.random.uniform(streams_of[7], (FF, D // 128), jnp.float32) ** block_scale(streams_of[7], (FF, D // 128), ((0, 32), (1, 8)), -0.2, 0.2)), 2.499999936844688e-05, 0.00025)
    return dict(prompt=prompt, dec_in=dec_in, gate_codes=gate_codes, gate_scale=gate_scale, up_codes=up_codes, up_scale=up_scale, down_codes=down_codes, down_scale=down_scale)


def dequant_rows(codes, scale):
    rows, cols = codes.shape
    full = codes.astype(jnp.float32).reshape(rows // 128, 128, cols) * scale[:, None, :]
    return full.reshape(rows, cols).astype(jnp.bfloat16)


def dequant_cols(codes, scale):
    rows, cols = codes.shape
    full = codes.astype(jnp.float32).reshape(rows, cols // 128, 128) * scale[:, :, None]
    return full.reshape(rows, cols).astype(jnp.bfloat16)


def block_sum(left, right, blocks):
    count, inner = left.shape
    width = inner // blocks
    left_blocks = left.reshape(count, blocks, width).transpose(1, 0, 2)
    right_blocks = right.reshape(blocks, width, right.shape[1])

    def add_block(total, pair):
        partial_value = jnp.dot(pair[0], pair[1], preferred_element_type=jnp.float32)
        rounded = lax.optimization_barrier(partial_value.astype(jnp.bfloat16))
        return total + rounded.astype(jnp.float32), None

    start = jnp.zeros((count, right.shape[1]), jnp.float32)
    total, _ = lax.scan(add_block, start, (left_blocks, right_blocks))
    return total


def reference(prompt, dec_in, gate_codes, gate_scale, up_codes, up_scale, down_codes, down_scale):
    gate_weight = dequant_rows(gate_codes, gate_scale)
    up_weight = dequant_rows(up_codes, up_scale)
    both_weights = jnp.concatenate([gate_weight, up_weight], axis=1)
    down_weight = dequant_cols(down_codes, down_scale)
    inputs = jnp.concatenate([prompt, dec_in.reshape(DEC_STEPS * DEC_ROWS, D)], axis=0)
    gate_up = block_sum(inputs, both_weights, N_GX)
    hidden = (jax.nn.silu(gate_up[:, :FF]) * gate_up[:, FF:]).astype(jnp.bfloat16)
    output = block_sum(hidden, down_weight, N_GY).astype(jnp.bfloat16)
    prompt_out = output[:PRE_TOK]
    dec_out = output[PRE_TOK:].reshape(DEC_STEPS, DEC_ROWS, D)
    return (prompt_out, dec_out)
```

```python
import jax
import jax.numpy as jnp
from jax import lax
from jax.experimental import pallas as pl
from jax.experimental.pallas import tpu as pltpu
from jax.sharding import PartitionSpec as P

MESH = pl.DeviceIdType.MESH
NX, NC, NY, NZ = 4, 2, 4, 8
BF, F32 = jnp.bfloat16, jnp.float32
ROWS = 256
CHUNKS = 4
GROUP = 16
PIECE = ROWS // (NX * NC)
HALF = ROWS // 2


def kernel(
    prompt, dec, gate, gate_scale, up, up_scale, down, down_scale,
    prompt_out, dec_out,
    w, sc, wd, ds, x_buf, dec_buf, p_buf, px_buf, q_buf, m1_buf, m2_buf, h_buf, o_buf, ry_buf, sy_buf, rz_buf,
    load_sem, own_sem, pr_send, pr_recv, dy_send, dy_recv, dz_send, dz_recv,
    ex_send, ex_recv, q_send, m1_recv, m2_recv, a_send, a_recv, c_send, c_recv, y_send, y_recv, z_send, z_recv,
):
    gx, gy = lax.axis_index("gx"), lax.axis_index("gy")
    x, c = gx // NC, lax.rem(gx, NC)
    y, z = gy // NZ, lax.rem(gy, NZ)
    width, ff = gate.shape
    half_of_z = lax.rem(z // 2, 2)
    slot_of_z = (z // 4) * 2 + lax.rem(z, 2)

    def at_gx(m):
        return (lax.rem(gx + m, NX * NC), gy)

    def at_x(m):
        return (lax.rem(x + m + NX, NX) * NC + c, gy)

    def at_y(m):
        return (gx, lax.rem(y + m, NY) * NZ + z)

    def at_z(m):
        return (gx, y * NZ + lax.rem(z + m, NZ))

    partner = (x * NC + 1 - c, gy)
    side = (at_x(-1), at_x(1))
    chip = (lax.rem(x + NX - 1, NX), lax.rem(x + 1, NX))
    across = lax.rem(x + 2, NX)

    def remote(src, dst, send, recv, where):
        return pltpu.make_async_remote_copy(
            src_ref=src, dst_ref=dst, send_sem=send, recv_sem=recv, device_id=where, device_id_type=MESH
        )

    loads = [
        pltpu.make_async_copy(gate, w.at[:, pl.ds(0, ff)], load_sem.at[0]),
        pltpu.make_async_copy(gate_scale, sc.at[:, pl.ds(0, ff)], load_sem.at[1]),
        pltpu.make_async_copy(up, w.at[:, pl.ds(ff, ff)], load_sem.at[2]),
        pltpu.make_async_copy(up_scale, sc.at[:, pl.ds(ff, ff)], load_sem.at[3]),
        pltpu.make_async_copy(dec, dec_buf, load_sem.at[4]),
        pltpu.make_async_copy(down, wd, load_sem.at[5]),
        pltpu.make_async_copy(down_scale, ds, load_sem.at[6]),
    ]
    loads[4].start()
    for i in (0, 1, 2, 3, 5, 6):
        loads[i].start()

    barrier = pltpu.get_barrier_semaphore()
    peers = [at_gx(m) for m in range(1, 8)] + [at_y(m) for m in range(1, 4)] + [at_z(m) for m in range(1, 8)]
    for peer in peers:
        pl.semaphore_signal(barrier, inc=1, device_id=peer, device_id_type=MESH)

    loads[4].wait()
    dec_rows = pl.ds(pl.multiple_of(slot_of_z * GROUP, GROUP), GROUP)
    x_buf[2 + half_of_z, y, dec_rows, :] = jnp.concatenate([dec_buf[0], dec_buf[1]], axis=0)
    pl.semaphore_wait(barrier, len(peers))

    prompt_rows = pl.ds(pl.multiple_of(c * 2 * GROUP, 2 * GROUP), 2 * GROUP)
    prompt_copies = []
    own_copies = []
    for h in range(2):
        src_rows = pl.ds(h * 2 * GROUP, 2 * GROUP)
        place = x_buf.at[h, x, prompt_rows, :]
        own = pltpu.make_async_copy(
            prompt.at[src_rows, pl.ds(pl.multiple_of(gx * width, width), width)], place, own_sem.at[h]
        )
        own.start()
        own_copies.append(own)
        group = []
        for m in range(1, 8):
            to = lax.rem(gx + m, NX * NC)
            copy = remote(
                prompt.at[src_rows, pl.ds(pl.multiple_of(to * width, width), width)],
                place, pr_send.at[h, m - 1], pr_recv.at[h, m - 1], at_gx(m),
            )
            copy.start()
            group.append(copy)
        prompt_copies.append(group)

    dec_block = x_buf.at[2 + half_of_z, y, dec_rows, :]
    dy_copies = []
    for m in range(1, 4):
        copy = remote(dec_block, dec_block, dy_send.at[m - 1], dy_recv.at[m - 1], at_y(m))
        copy.start()
        dy_copies.append(copy)

    def dequant_gate_up():
        for i in (0, 1, 2, 3):
            loads[i].wait()

        def tile(j, carry):
            cols = pl.ds(pl.multiple_of(j * 256, 256), 256)
            for r in range(8):
                rows = pl.ds(r * 128, 128)
                w[rows, cols] = (w[rows, cols].astype(F32) * sc[pl.ds(r, 1), cols]).astype(BF)
            return carry

        lax.fori_loop(0, 2 * ff // 256, tile, 0)

    def dequant_down():
        for i in (5, 6):
            loads[i].wait()

        def tile(j, carry):
            rows = pl.ds(pl.multiple_of(j * 128, 128), 128)
            for b in range(8):
                cols = pl.ds(b * 128, 128)
                wd[rows, cols] = (wd[rows, cols].astype(F32) * ds[rows, pl.ds(b, 1)]).astype(BF)
            return carry

        lax.fori_loop(0, ff // 128, tile, 0)

    dz_copies = []

    def decode_z():
        for copy in dy_copies:
            copy.wait_recv()
        column = x_buf.at[2 + half_of_z, :, dec_rows, :]
        for m in range(1, 8):
            copy = remote(column, column, dz_send.at[m - 1], dz_recv.at[m - 1], at_z(m))
            copy.start()
            dz_copies.append(copy)

    def wait_input(k):
        if k < 2:
            own_copies[k].wait()
            for copy in prompt_copies[k]:
                copy.wait_recv()
        elif k == 2:
            for copy in dz_copies:
                copy.wait_recv()

    theirs = pl.ds(pl.multiple_of((1 - c) * HALF, HALF), HALF)

    def exchange(k):
        return remote(p_buf.at[k, theirs, :], px_buf.at[k], ex_send.at[k], ex_recv.at[k], partner)

    def stage1(k):
        def tile(j, carry):
            cols = pl.ds(pl.multiple_of(j * 256, 256), 256)
            product = jnp.dot(x_buf[k].reshape(ROWS, width), w[:, cols], preferred_element_type=F32)
            p_buf[k, :, cols] = product.astype(BF)
            remote(
                p_buf.at[k, theirs, cols], px_buf.at[k, :, cols], ex_send.at[k], ex_recv.at[k], partner
            ).start()
            return carry

        lax.fori_loop(0, 2 * ff // 256, tile, 0)

    def own_rows(start):
        return pl.ds(pl.multiple_of(c * HALF + start, GROUP), GROUP)

    def px_rows(start):
        return pl.ds(pl.multiple_of(start, GROUP), GROUP)

    def pair_sum(k, start, cols):
        return p_buf[k, own_rows(start), cols].astype(F32) + px_buf[k, px_rows(start), cols].astype(F32)

    def columns(n, step, fn):
        def tile(j, carry):
            fn(pl.multiple_of(j * step, step))
            return carry

        lax.fori_loop(0, n // step, tile, 0)

    pending = []

    def q_copy(k, kind, d):
        src = q_buf.at[k, kind, d]
        if kind == 0:
            return remote(src, m1_buf.at[k, d], q_send.at[k, 0, d], m1_recv.at[k, d], side[d])
        half = 1 - d if kind == 1 else d
        return remote(
            src, m2_buf.at[k, d, pl.ds(half * GROUP, GROUP), :],
            q_send.at[k, kind, d], m2_recv.at[k, kind - 1, d], side[d],
        )

    def send(copy):
        copy.start()
        pending.append(copy)

    def stage2(k):
        exchange(k).wait_recv()
        for kind in (0, 1):
            starts = [(across * PIECE + d * GROUP) if kind == 0 else (chip[d] * PIECE + (1 - d) * GROUP) for d in (0, 1)]

            def fn(j):
                cols = pl.ds(j, 256)
                for d in (0, 1):
                    q_buf[k, kind, d, :, cols] = pair_sum(k, starts[d], cols).astype(BF)

            columns(2 * ff, 256, fn)
            for d in (0, 1):
                send(q_copy(k, kind, d))

    def stage3(k):
        for d in (0, 1):
            q_copy(k, 0, d).wait_recv()

        def fn(j):
            cols = pl.ds(j, 256)
            for d in (0, 1):
                total = pair_sum(k, chip[d] * PIECE + d * GROUP, cols) + m1_buf[k, d, :, cols].astype(F32)
                q_buf[k, 2, d, :, cols] = total.astype(BF)

        columns(2 * ff, 256, fn)
        for d in (0, 1):
            send(q_copy(k, 2, d))

    def piece_rows(core, at, start=0, size=PIECE):
        return pl.ds(pl.multiple_of(core * HALF + at * PIECE + start, GROUP), size)

    def a_copy(k, step, d):
        if step == 0:
            part = h_buf.at[k, piece_rows(c, x), :]
        else:
            part = h_buf.at[k, piece_rows(c, chip[1 - d], d * GROUP, GROUP), :]
        return remote(part, part, a_send.at[k, step, d], a_recv.at[k, step, d], side[d])

    def c_copy(k, i):
        at = (x, chip[0], chip[1], across)[i]
        part = h_buf.at[k, piece_rows(c, at), :]
        return remote(part, part, c_send.at[k, i], c_recv.at[k, i], partner)

    def stage4(k):
        for kind in (1, 2):
            for d in (0, 1):
                q_copy(k, kind, d).wait_recv()

        def fn(j):
            for r in (0, GROUP):
                values = []
                for first in (0, ff):
                    cols = pl.ds(pl.multiple_of(first + j, 128), 128)
                    total = pair_sum(k, x * PIECE + r, cols)
                    for d in (0, 1):
                        total = total + m2_buf[k, d, pl.ds(r, GROUP), cols].astype(F32)
                    values.append(total)
                g, u = values
                rows = pl.ds(pl.multiple_of(c * HALF + x * PIECE + r, GROUP), GROUP)
                h_buf[k, rows, pl.ds(j, 128)] = (g / (1.0 + jnp.exp(-g)) * u).astype(BF)

        columns(ff, 128, fn)
        for d in (0, 1):
            send(a_copy(k, 0, d))
        send(c_copy(k, 0))

    def stage5(k):
        for d in (0, 1):
            a_copy(k, 0, d).wait_recv()
        for d in (0, 1):
            send(a_copy(k, 1, d))
        send(c_copy(k, 1))
        send(c_copy(k, 2))

    def stage6(k):
        for d in (0, 1):
            a_copy(k, 1, d).wait_recv()
        send(c_copy(k, 3))

    def y_copy(k, m):
        return remote(
            o_buf.at[k, lax.rem(y + m, NY)], ry_buf.at[k, m - 1], y_send.at[k, m - 1], y_recv.at[k, m - 1], at_y(m)
        )

    def stage7(k):
        for i in range(4):
            c_copy(k, i).wait_recv()

        def tile(j, carry):
            cols = pl.ds(pl.multiple_of(j * 256, 256), 256)
            product = jnp.dot(h_buf[k], wd[:, cols], preferred_element_type=F32)
            o_buf[k, :, :, cols] = product.astype(BF).reshape(NY, ROWS // NY, 256)
            return carry

        lax.fori_loop(0, width // 256, tile, 0)
        for m in range(1, 4):
            send(y_copy(k, m))

    def z_copy(k, i):
        to = (i // 2) * 4 + (k % 2) * 2 + i % 2
        m = lax.rem(to - z + NZ, NZ)
        slot = lax.rem(m + NZ - 1, NZ)
        return to, remote(
            sy_buf.at[k, pl.ds(i * GROUP, GROUP), :], rz_buf.at[k // 2, slot],
            z_send.at[k, i], z_recv.at[k // 2, slot], (gx, y * NZ + to),
        )

    def stage8(k):
        for m in range(1, 4):
            y_copy(k, m).wait_recv()

        def fn(j):
            cols = pl.ds(j, 256)
            total = o_buf[k, y, :, cols].astype(F32)
            for m in range(3):
                total = total + ry_buf[k, m, :, cols].astype(F32)
            sy_buf[k, :, cols] = total.astype(BF)

        columns(width, 256, fn)
        for i in range(4):
            to, copy = z_copy(k, i)

            @pl.when(to != z)
            def _():
                copy.start()

    def stage9(kind):
        for m in range(NZ - 1):
            slot = rz_buf.at[kind, m]
            remote(slot, slot, z_send.at[0, 0], z_recv.at[kind, m], at_z(1)).wait_recv()
        rows = pl.ds(pl.multiple_of(slot_of_z * GROUP, GROUP), GROUP)
        k = kind * 2 + half_of_z
        for j in range(0, width, 256):
            cols = pl.ds(j, 256)
            total = sy_buf[k, rows, cols].astype(F32)
            for m in range(NZ - 1):
                total = total + rz_buf[kind, m, :, cols].astype(F32)
            total = total.astype(BF)
            if kind == 0:
                prompt_out[:, cols] = total
            else:
                dec_out[0, :, cols] = total[0:8]
                dec_out[1, :, cols] = total[8:16]

    dequant_gate_up()
    decode_z()
    wait_input(0)
    stage1(0)
    stage2(0)
    wait_input(1)
    stage1(1)
    dequant_down()
    stage3(0)
    stage2(1)
    stage4(0)
    wait_input(2)
    stage1(2)
    stage3(1)
    stage2(2)
    stage5(0)
    stage4(1)
    stage6(0)
    stage1(3)
    stage3(2)
    stage2(3)
    stage7(0)
    stage5(1)
    stage4(2)
    stage6(1)
    stage8(0)
    stage3(3)
    stage7(1)
    stage5(2)
    stage4(3)
    stage6(2)
    stage8(1)
    stage5(3)
    stage7(2)
    stage6(3)
    stage9(0)
    stage8(2)
    stage7(3)
    stage8(3)
    stage9(1)

    for group in prompt_copies:
        for copy in group:
            copy.wait_send()
    for copy in dy_copies + dz_copies + pending:
        copy.wait_send()
    for k in range(CHUNKS):
        exchange(k).wait_send()
        for i in range(4):
            to, copy = z_copy(k, i)

            @pl.when(to != z)
            def _():
                copy.wait_send()


def body(prompt, dec_in, gate_codes, gate_scale, up_codes, up_scale, down_codes, down_scale):
    width, ff = gate_codes.shape
    dma = pltpu.SemaphoreType.DMA
    any_spec = pl.BlockSpec(memory_space=pl.ANY)
    vmem = pl.BlockSpec(memory_space=pltpu.VMEM)
    return pl.pallas_call(
        kernel,
        out_shape=(
            jax.ShapeDtypeStruct((GROUP, width), BF),
            jax.ShapeDtypeStruct(dec_in.shape, BF),
        ),
        in_specs=[any_spec] * 8,
        out_specs=(vmem, vmem),
        scratch_shapes=[
            pltpu.VMEM((width, 2 * ff), BF),
            pltpu.VMEM((8, 2 * ff), F32),
            pltpu.VMEM((ff, width), BF),
            pltpu.VMEM((ff, 8), F32),
            pltpu.VMEM((CHUNKS, NY, ROWS // NY, width), BF),
            pltpu.VMEM(dec_in.shape, BF),
            pltpu.VMEM((CHUNKS, ROWS, 2 * ff), BF),
            pltpu.VMEM((CHUNKS, HALF, 2 * ff), BF),
            pltpu.VMEM((CHUNKS, 3, 2, GROUP, 2 * ff), BF),
            pltpu.VMEM((CHUNKS, 2, GROUP, 2 * ff), BF),
            pltpu.VMEM((CHUNKS, 2, PIECE, 2 * ff), BF),
            pltpu.VMEM((CHUNKS, ROWS, ff), BF),
            pltpu.VMEM((CHUNKS, NY, ROWS // NY, width), BF),
            pltpu.VMEM((CHUNKS, 3, ROWS // NY, width), BF),
            pltpu.VMEM((CHUNKS, ROWS // NY, width), BF),
            pltpu.VMEM((2, NZ - 1, GROUP, width), BF),
            dma((7,)),
            dma((2,)),
            dma((2, 7)),
            dma((2, 7)),
            dma((3,)),
            dma((3,)),
            dma((7,)),
            dma((7,)),
            dma((CHUNKS,)),
            dma((CHUNKS,)),
            dma((CHUNKS, 3, 2)),
            dma((CHUNKS, 2)),
            dma((CHUNKS, 2, 2)),
            dma((CHUNKS, 2, 2)),
            dma((CHUNKS, 2, 2)),
            dma((CHUNKS, 4)),
            dma((CHUNKS, 4)),
            dma((CHUNKS, 3)),
            dma((CHUNKS, 3)),
            dma((CHUNKS, 4)),
            dma((2, NZ - 1)),
        ],
        compiler_params=pltpu.CompilerParams(
            collective_id=0, has_side_effects=True, vmem_limit_bytes=60 * 1024 * 1024
        ),
        cost_estimate=pl.CostEstimate(flops=10_500_000_000, bytes_accessed=12_000_000, transcendentals=1_000_000),
        name="ffn",
    )(prompt, dec_in, gate_codes, gate_scale, up_codes, up_scale, down_codes, down_scale)


def solution(mesh):
    in_specs = (
        P("gx", None),
        P(None, "gy", "gx"),
        P("gx", "gy"),
        P("gx", "gy"),
        P("gx", "gy"),
        P("gx", "gy"),
        P("gy", "gx"),
        P("gy", "gx"),
    )
    out_specs = (P("gy", "gx"), P(None, "gy", "gx"))
    return jax.shard_map(body, mesh=mesh, in_specs=in_specs, out_specs=out_specs, check_vma=False)
```

```python
import jax
import jax.numpy as jnp
from jax import lax
from jax.experimental import pallas as pl
from jax.experimental.pallas import tpu as pltpu
from jax.sharding import PartitionSpec as P

MESH = pl.DeviceIdType.MESH
NX, NC, NY, NZ = 4, 2, 4, 8
BF, F32 = jnp.bfloat16, jnp.float32
GROUP = 16
NQ = 4
ROWS = NY * 2 * GROUP
CHUNKS = 2 * NQ
PIECE = ROWS // (NX * NC)
HALF = ROWS // 2
DIRECT = 2
DEQ = 4

OFFSETS = (0, 0.5, 1.65, 3.1, 4.4, 5.8, 6.2, 8.7)


def stage_order():
    steps = [(k + at, -i, i, k) for k in range(CHUNKS) for i, at in enumerate(OFFSETS)]
    return [(i, k) for _, _, i, k in sorted(steps)]


def kernel(
    prompt, dec, gate, gate_scale, up, up_scale, down, down_scale,
    prompt_out, dec_out,
    w, sc, wd, ds, x_buf, pb_buf, dec_buf, p_buf, px_buf, q_buf, m1_buf, m2_buf, h_buf, o_buf, ry_buf, sy_buf, rz_buf,
    load_sem, down_sem, dec_sem, own_sem, pc_send, pc_recv, px_send, px_recv, py_send, py_recv, dz_send, dz_recv, dy_send, dy_recv,
    ex_send, ex_recv, q_send, m1_recv, m2_recv, a_send, a_recv, c_send, c_recv, y_send, y_recv, z_send, z_recv,
):
    gx, gy = lax.axis_index("gx"), lax.axis_index("gy")
    x, c = gx // NC, lax.rem(gx, NC)
    y, z = gy // NZ, lax.rem(gy, NZ)
    width, ff = gate.shape
    my_q, my_zh = lax.rem(z, NQ), z // NQ

    def chip_at(m):
        return lax.rem(x + m, NX)

    def at_x(m):
        return (chip_at(m) * NC + c, gy)

    def at_y(m):
        return (gx, lax.rem(y + m, NY) * NZ + z)

    def at_z(m):
        return (gx, y * NZ + lax.rem(z + m, NZ))

    partner = (x * NC + 1 - c, gy)
    side = (at_x(NX - 1), at_x(1))
    chip = (chip_at(NX - 1), chip_at(1))
    across = chip_at(2)

    def remote(src, dst, send, recv, where):
        return pltpu.make_async_remote_copy(
            src_ref=src, dst_ref=dst, send_sem=send, recv_sem=recv, device_id=where, device_id_type=MESH
        )

    pending = []

    def send(copy):
        copy.start()
        pending.append(copy)

    dec_load = pltpu.make_async_copy(dec, dec_buf, dec_sem.at[0])
    dec_load.start()
    part = width // DEQ
    loads = []
    for i in range(DEQ):
        rows, scales = pl.ds(i * part, part), pl.ds(i * part // 128, part // 128)
        if i == 0:
            loads.append([
                pltpu.make_async_copy(gate_scale, sc.at[:, pl.ds(0, ff)], load_sem.at[DEQ, 0]),
                pltpu.make_async_copy(up_scale, sc.at[:, pl.ds(ff, ff)], load_sem.at[DEQ, 1]),
            ])
        else:
            loads.append([])
        loads[i].append(pltpu.make_async_copy(gate.at[rows, :], w.at[rows, pl.ds(0, ff)], load_sem.at[i, 0]))
        loads[i].append(pltpu.make_async_copy(up.at[rows, :], w.at[rows, pl.ds(ff, ff)], load_sem.at[i, 1]))
        for load in loads[i]:
            load.start()
    down_loads = [
        pltpu.make_async_copy(down, wd, down_sem.at[0]),
        pltpu.make_async_copy(down_scale, ds, down_sem.at[1]),
    ]
    for load in down_loads:
        load.start()

    barrier = pltpu.get_barrier_semaphore()
    peers = [partner] + [at_x(m) for m in range(1, NX)]
    peers += [at_y(m) for m in range(1, NY)] + [at_z(m) for m in range(1, NZ)]
    for peer in peers:
        pl.semaphore_signal(barrier, inc=1, device_id=peer, device_id_type=MESH)

    dec_load.wait()
    x_buf[1, my_q, y, my_zh] = jnp.concatenate([dec_buf[0], dec_buf[1]], axis=0)
    pl.semaphore_wait(barrier, len(peers))

    share = width // NY

    def prompt_cols(q):
        if q < DIRECT:
            return pl.ds(0, width)
        return pl.ds(pl.multiple_of(y * share, share), share)

    def prompt_part(q, m, core):
        size = width if q < DIRECT else share
        first = (chip_at(m) * NC + core) * width + (0 if q < DIRECT else y * share)
        return prompt.at[q, :, pl.ds(pl.multiple_of(first, share), size)]

    def prompt_place(q, core):
        return x_buf.at[0, q, x, core, :, prompt_cols(q)]

    def prompt_core(q, m):
        dst = prompt_place(q, c) if m == 0 else pb_buf.at[q, m - 1, :, prompt_cols(q)]
        return remote(prompt_part(q, m, 1 - c), dst, pc_send.at[q, m], pc_recv.at[q, m], partner)

    def prompt_x(q, m, core):
        src = prompt_part(q, m, c) if core == 0 else pb_buf.at[q, m - 1, :, prompt_cols(q)]
        dst = prompt_place(q, c if core == 0 else 1 - c)
        return remote(src, dst, px_send.at[q, m - 1, core], px_recv.at[q, m - 1, core], at_x(m))

    def prompt_own(q):
        return pltpu.make_async_copy(prompt_part(q, 0, c), prompt_place(q, c), own_sem.at[q])

    def prompt_y(q, m):
        block = x_buf.at[0, q, :, :, :, prompt_cols(q)]
        return remote(block, block, py_send.at[q, m - 1], py_recv.at[q, m - 1], at_y(m))

    def prompt_start(q):
        prompt_own(q).start()
        for m in (2, 1, 3):
            send(prompt_x(q, m, 0))

    def prompt_forward(q):
        for m in (2, 1, 3):
            prompt_core(q, m).wait_recv()
            send(prompt_x(q, m, 1))

    def prompt_along_x(q):
        prompt_own(q).wait()
        prompt_core(q, 0).wait_recv()
        for m in (1, 3, 2):
            for core in (0, 1):
                prompt_x(q, m, core).wait_recv()

    def prompt_along_y(q):
        prompt_along_x(q)
        for m in (2, 1, 3):
            send(prompt_y(q, m))

    dec_block = x_buf.at[1, my_q, y, my_zh]
    for q in range(NQ):
        for m in (2, 1, 3, 0):
            send(prompt_core(q, m))
        if q == 0:
            prompt_start(0)
            for m in (4, 3, 5, 2, 6, 1, 7):
                send(remote(dec_block, dec_block, dz_send.at[m - 1], dz_recv.at[z], at_z(m)))
    prompt_forward(0)
    for q in range(DIRECT, NQ):
        prompt_start(q)
        prompt_forward(q)
    for q in range(1, DIRECT):
        prompt_start(q)
        prompt_forward(q)

    def decode_y(q):
        for zh in (0, 1):
            block = x_buf.at[1, q, y, zh]

            @pl.when(z != zh * NQ + q)
            def _():
                remote(block, block, dz_send.at[0], dz_recv.at[zh * NQ + q], at_z(1)).wait_recv()

        for m in (1, 3, 2):
            send(decode_y_copy(q, m))

    def decode_y_copy(q, m):
        block = x_buf.at[1, q, y]
        return remote(block, block, dy_send.at[q, m - 1], dy_recv.at[q, m - 1], at_y(m))

    def wait_input(k):
        if k < DIRECT:
            prompt_along_x(k)
        elif k < NQ:
            for m in (1, 3, 2):
                prompt_y(k, m).wait_recv()
        else:
            for m in (1, 3, 2):
                decode_y_copy(k - NQ, m).wait_recv()

    def dequant_gate_up(i):
        for load in loads[i]:
            load.wait()

        def tile(j, carry):
            cols = pl.ds(pl.multiple_of(j * 256, 256), 256)
            for r in range(i * part // 128, (i + 1) * part // 128):
                rows = pl.ds(r * 128, 128)
                w[rows, cols] = (w[rows, cols].astype(F32) * sc[pl.ds(r, 1), cols]).astype(BF)
            return carry

        lax.fori_loop(0, 2 * ff // 256, tile, 0)

    def dequant_down():
        for load in down_loads:
            load.wait()

        def tile(j, carry):
            rows = pl.ds(pl.multiple_of(j * 128, 128), 128)
            scales = ds[:, rows].T
            for b in range(8):
                cols = pl.ds(b * 128, 128)
                wd[rows, cols] = (wd[rows, cols].astype(F32) * scales[:, b : b + 1]).astype(BF)
            return carry

        lax.fori_loop(0, ff // 128, tile, 0)

    theirs = pl.ds(pl.multiple_of((1 - c) * HALF, HALF), HALF)
    sides = (pl.ds(0, ff), pl.ds(ff, ff))

    def exchange(k, s):
        return remote(
            p_buf.at[k, theirs, sides[s]], px_buf.at[k, :, sides[s]], ex_send.at[k, s], ex_recv.at[k, s], partner
        )

    def stage1(k):
        wait_input(k)
        rows = x_buf[k // NQ, k % NQ].reshape(ROWS, width)
        for s in (0, 1):
            p_buf[k, :, sides[s]] = jnp.dot(rows, w[:, sides[s]], preferred_element_type=F32).astype(BF)
            send(exchange(k, s))

    def pair_sum(k, at, s):
        own = pl.ds(pl.multiple_of(c * HALF + at * PIECE, PIECE), PIECE)
        got = pl.ds(pl.multiple_of(at * PIECE, PIECE), PIECE)
        return p_buf[k, own, sides[s]].astype(F32) + px_buf[k, got, sides[s]].astype(F32)

    def q_copy(k, kind, d):
        src = q_buf.at[k, kind, d]
        if kind == 0:
            return remote(src, m1_buf.at[k, d], q_send.at[k, 0, d], m1_recv.at[k, d], side[d])
        s = 1 - d if kind == 1 else d
        return remote(src, m2_buf.at[k, d, s], q_send.at[k, kind, d], m2_recv.at[k, kind - 1, d], side[d])

    def stage2(k):
        for s in (0, 1):
            exchange(k, s).wait_recv()
        for kind in (0, 1):
            for d in (0, 1):
                at, s = (across, d) if kind == 0 else (chip[d], 1 - d)
                q_buf[k, kind, d] = pair_sum(k, at, s).astype(BF)
                send(q_copy(k, kind, d))

    def stage3(k):
        for d in (0, 1):
            q_copy(k, 0, d).wait_recv()
            q_buf[k, 2, d] = (pair_sum(k, chip[d], d) + m1_buf[k, d].astype(F32)).astype(BF)
            send(q_copy(k, 2, d))

    def piece(k, core, at, cols=pl.ds(0, 1664)):
        return h_buf.at[k, pl.ds(pl.multiple_of(core * HALF + at * PIECE, PIECE), PIECE), cols]

    cut = ff // 256 * 128 + 128
    cuts = (pl.ds(0, cut), pl.ds(cut, ff - cut))

    def a_copy(k, step, d):
        block = piece(k, c, x) if step == 0 else piece(k, c, chip[1 - d], cuts[d])
        return remote(block, block, a_send.at[k, step, d], a_recv.at[k, step, d], side[d])

    def c_copy(k, i):
        block = piece(k, c, (x, chip[0], chip[1], across)[i])
        return remote(block, block, c_send.at[k, i], c_recv.at[k, i], partner)

    def stage4(k):
        for kind in (1, 2):
            for d in (0, 1):
                q_copy(k, kind, d).wait_recv()
        g, u = [
            pair_sum(k, x, s) + m2_buf[k, 0, s].astype(F32) + m2_buf[k, 1, s].astype(F32) for s in (0, 1)
        ]
        own = pl.ds(pl.multiple_of(c * HALF + x * PIECE, PIECE), PIECE)
        h_buf[k, own, :] = (g / (1.0 + jnp.exp(-g)) * u).astype(BF)
        for d in (0, 1):
            send(a_copy(k, 0, d))
        send(c_copy(k, 0))

    def stage5(k):
        for d in (0, 1):
            a_copy(k, 0, d).wait_recv()
            send(a_copy(k, 1, d))
        send(c_copy(k, 1))
        send(c_copy(k, 2))

    def stage6(k):
        for d in (0, 1):
            a_copy(k, 1, d).wait_recv()
        send(c_copy(k, 3))

    def y_copy(k, m):
        return remote(
            o_buf.at[k, lax.rem(y + m, NY)], ry_buf.at[k, m - 1], y_send.at[k, m - 1], y_recv.at[k, m - 1], at_y(m)
        )

    def stage7(k):
        for i in range(4):
            c_copy(k, i).wait_recv()
        product = jnp.dot(h_buf[k], wd[...], preferred_element_type=F32)
        o_buf[k] = product.astype(BF).reshape(NY, ROWS // NY, width)
        for m in (1, 3, 2):
            send(y_copy(k, m))

    def z_copy(k, zh):
        to = zh * NQ + k % NQ
        slot = lax.rem(to - z + 2 * NZ - 1, NZ)
        return to, remote(
            sy_buf.at[k, pl.ds(zh * GROUP, GROUP), :], rz_buf.at[k // NQ, slot],
            z_send.at[k, zh], z_recv.at[k // NQ, slot], (gx, y * NZ + to),
        )

    def stage8(k):
        for m in (1, 3, 2):
            y_copy(k, m).wait_recv()
        for j in range(0, width, 256):
            cols = pl.ds(j, 256)
            total = o_buf[k, y, :, cols].astype(F32)
            for m in range(3):
                total = total + ry_buf[k, m, :, cols].astype(F32)
            sy_buf[k, :, cols] = total.astype(BF)
        for zh in (0, 1):
            to, copy = z_copy(k, zh)

            @pl.when(to != z)
            def _():
                copy.start()

    def finish(kind):
        for m in range(NZ - 1):
            slot = rz_buf.at[kind, m]
            remote(slot, slot, z_send.at[0, 0], z_recv.at[kind, m], at_z(1)).wait_recv()
        rows = pl.ds(pl.multiple_of(my_zh * GROUP, GROUP), GROUP)
        for j in range(0, width, 256):
            cols = pl.ds(j, 256)
            total = sy_buf[kind * NQ + my_q, rows, cols].astype(F32)
            for m in range(NZ - 1):
                total = total + rz_buf[kind, m, :, cols].astype(F32)
            total = total.astype(BF)
            if kind == 0:
                prompt_out[:, cols] = total
            else:
                dec_out[0, :, cols] = total[0:8]
                dec_out[1, :, cols] = total[8:16]

    stages = (stage1, stage2, stage3, stage4, stage5, stage6, stage7, stage8)
    for i in range(DEQ):
        dequant_gate_up(i)
    for q in range(DIRECT, NQ):
        prompt_along_y(q)
    for i, k in stage_order():
        if (i, k) == (1, 0):
            for q in range(NQ):
                decode_y(q)
        if (i, k) == (1, 1):
            dequant_down()
        stages[i](k)
    finish(0)
    finish(1)

    for copy in pending:
        copy.wait_send()
    for k in range(CHUNKS):
        for zh in (0, 1):
            to, copy = z_copy(k, zh)

            @pl.when(to != z)
            def _():
                copy.wait_send()


def body(prompt, dec_in, gate_codes, gate_scale, up_codes, up_scale, down_codes, down_scale):
    width, ff = gate_codes.shape
    dma = pltpu.SemaphoreType.DMA
    any_spec = pl.BlockSpec(memory_space=pl.ANY)
    vmem = pl.BlockSpec(memory_space=pltpu.VMEM)
    return pl.pallas_call(
        kernel,
        out_shape=(
            jax.ShapeDtypeStruct((GROUP, width), BF),
            jax.ShapeDtypeStruct(dec_in.shape, BF),
        ),
        in_specs=[any_spec] * 8,
        out_specs=(vmem, vmem),
        scratch_shapes=[
            pltpu.VMEM((width, 2 * ff), BF),
            pltpu.VMEM((8, 2 * ff), F32),
            pltpu.VMEM((ff, width), BF),
            pltpu.VMEM((8, ff), F32),
            pltpu.VMEM((2, NQ, NY, 2, GROUP, width), BF),
            pltpu.VMEM((NQ, NX - 1, GROUP, width), BF),
            pltpu.VMEM(dec_in.shape, BF),
            pltpu.VMEM((CHUNKS, ROWS, 2 * ff), BF),
            pltpu.VMEM((CHUNKS, HALF, 2 * ff), BF),
            pltpu.VMEM((CHUNKS, 3, 2, PIECE, ff), BF),
            pltpu.VMEM((CHUNKS, 2, PIECE, ff), BF),
            pltpu.VMEM((CHUNKS, 2, 2, PIECE, ff), BF),
            pltpu.VMEM((CHUNKS, ROWS, ff), BF),
            pltpu.VMEM((CHUNKS, NY, ROWS // NY, width), BF),
            pltpu.VMEM((CHUNKS, 3, ROWS // NY, width), BF),
            pltpu.VMEM((CHUNKS, ROWS // NY, width), BF),
            pltpu.VMEM((2, NZ - 1, GROUP, width), BF),
            dma((DEQ + 1, 2)),
            dma((2,)),
            dma((1,)),
            dma((NQ,)),
            dma((NQ, NX)),
            dma((NQ, NX)),
            dma((NQ, NX - 1, 2)),
            dma((NQ, NX - 1, 2)),
            dma((NQ, NY - 1)),
            dma((NQ, NY - 1)),
            dma((NZ - 1,)),
            dma((NZ,)),
            dma((NQ, NY - 1)),
            dma((NQ, NY - 1)),
            dma((CHUNKS, 2)),
            dma((CHUNKS, 2)),
            dma((CHUNKS, 3, 2)),
            dma((CHUNKS, 2)),
            dma((CHUNKS, 2, 2)),
            dma((CHUNKS, 2, 2)),
            dma((CHUNKS, 2, 2)),
            dma((CHUNKS, 4)),
            dma((CHUNKS, 4)),
            dma((CHUNKS, 3)),
            dma((CHUNKS, 3)),
            dma((CHUNKS, 2)),
            dma((2, NZ - 1)),
        ],
        compiler_params=pltpu.CompilerParams(
            collective_id=0, has_side_effects=True, vmem_limit_bytes=60 * 1024 * 1024
        ),
        cost_estimate=pl.CostEstimate(flops=10_500_000_000, bytes_accessed=12_000_000, transcendentals=1_000_000),
        name="ffn",
    )(
        prompt.reshape(NQ, GROUP, prompt.shape[1]), dec_in, gate_codes, gate_scale, up_codes, up_scale, down_codes,
        down_scale.T,
    )


def solution(mesh):
    in_specs = (
        P("gx", None),
        P(None, "gy", "gx"),
        P("gx", "gy"),
        P("gx", "gy"),
        P("gx", "gy"),
        P("gx", "gy"),
        P("gy", "gx"),
        P("gy", "gx"),
    )
    out_specs = (P("gy", "gx"), P(None, "gy", "gx"))
    return jax.shard_map(body, mesh=mesh, in_specs=in_specs, out_specs=out_specs, check_vma=False)
```

```python
import jax
import jax.numpy as jnp
from jax import lax
from jax.experimental import pallas as pl
from jax.experimental.pallas import tpu as pltpu
from jax.sharding import PartitionSpec as P

MESH = pl.DeviceIdType.MESH
NX, NC, NY, NZ = 4, 2, 4, 8
BF, F32 = jnp.bfloat16, jnp.float32
GROUP = 16
NQ = 4
ROWS = NY * 2 * GROUP
CHUNKS = 2 * NQ
PIECE = ROWS // (NX * NC)
HALF = ROWS // 2
DIRECT = 2
DEQ = 4

OFFSETS = (0, 0.5, 1.65, 3.1, 4.4, 5.8, 6.2, 8.7)


def stage_order():
    steps = [(k + at, -i, i, k) for k in range(CHUNKS) for i, at in enumerate(OFFSETS)]
    return [(i, k) for _, _, i, k in sorted(steps)]


def kernel(
    prompt, dec, gate, gate_scale, up, up_scale, down, down_scale,
    out,
    w, sc, wd, ds, x_buf, pb_buf, dec_buf, p_buf, px_buf, q_buf, m1_buf, m2_buf, h_buf, o_buf, ry_buf, sy_buf, rz_buf,
    load_sem, down_sem, dec_sem, own_sem, pc_send, pc_recv, px_send, px_recv, py_send, py_recv, dz_send, dz_recv, dy_send, dy_recv,
    ex_send, ex_recv, q_send, m1_recv, m2_recv, a_send, a_recv, c_send, c_recv, y_send, y_recv, z_send, z_recv,
):
    gx, gy = lax.axis_index("gx"), lax.axis_index("gy")
    x, c = gx // NC, lax.rem(gx, NC)
    y, z = gy // NZ, lax.rem(gy, NZ)
    width, ff = gate.shape
    my_q, my_zh = lax.rem(z, NQ), z // NQ

    def chip_at(m):
        return lax.rem(x + m, NX)

    def at_x(m):
        return (chip_at(m) * NC + c, gy)

    def at_y(m):
        return (gx, lax.rem(y + m, NY) * NZ + z)

    def at_z(m):
        return (gx, y * NZ + lax.rem(z + m, NZ))

    partner = (x * NC + 1 - c, gy)
    side = (at_x(NX - 1), at_x(1))
    chip = (chip_at(NX - 1), chip_at(1))
    across = chip_at(2)

    def remote(src, dst, send, recv, where):
        return pltpu.make_async_remote_copy(
            src_ref=src, dst_ref=dst, send_sem=send, recv_sem=recv, device_id=where, device_id_type=MESH
        )

    pending = []

    def send(copy):
        copy.start()
        pending.append(copy)

    dec_load = pltpu.make_async_copy(dec, dec_buf, dec_sem.at[0])
    dec_load.start()
    part = width // DEQ
    loads = []
    for i in range(DEQ):
        rows, scales = pl.ds(i * part, part), pl.ds(i * part // 128, part // 128)
        if i == 0:
            loads.append([
                pltpu.make_async_copy(gate_scale, sc.at[:, pl.ds(0, ff)], load_sem.at[DEQ, 0]),
                pltpu.make_async_copy(up_scale, sc.at[:, pl.ds(ff, ff)], load_sem.at[DEQ, 1]),
            ])
        else:
            loads.append([])
        loads[i].append(pltpu.make_async_copy(gate.at[rows, :], w.at[rows, pl.ds(0, ff)], load_sem.at[i, 0]))
        loads[i].append(pltpu.make_async_copy(up.at[rows, :], w.at[rows, pl.ds(ff, ff)], load_sem.at[i, 1]))
        for load in loads[i]:
            load.start()
    down_loads = [
        pltpu.make_async_copy(down, wd, down_sem.at[0]),
        pltpu.make_async_copy(down_scale, ds, down_sem.at[1]),
    ]

    barrier = pltpu.get_barrier_semaphore()
    peers = [partner] + [at_x(m) for m in range(1, NX)]
    peers += [at_y(m) for m in range(1, NY)] + [at_z(m) for m in range(1, NZ)]
    for peer in peers:
        pl.semaphore_signal(barrier, inc=1, device_id=peer, device_id_type=MESH)

    dec_load.wait()
    x_buf[1, my_q, y, my_zh] = jnp.concatenate([dec_buf[0], dec_buf[1]], axis=0)
    pl.semaphore_wait(barrier, len(peers))

    share = width // NY

    def prompt_cols(q):
        if q < DIRECT:
            return pl.ds(0, width)
        return pl.ds(pl.multiple_of(y * share, share), share)

    def prompt_part(q, m, core):
        size = width if q < DIRECT else share
        first = (chip_at(m) * NC + core) * width + (0 if q < DIRECT else y * share)
        return prompt.at[q, :, pl.ds(pl.multiple_of(first, share), size)]

    def prompt_place(q, core):
        return x_buf.at[0, q, x, core, :, prompt_cols(q)]

    def prompt_core(q, m):
        dst = prompt_place(q, c) if m == 0 else pb_buf.at[q, m - 1, :, prompt_cols(q)]
        return remote(prompt_part(q, m, 1 - c), dst, pc_send.at[q, m], pc_recv.at[q, m], partner)

    def prompt_x(q, m, core):
        src = prompt_part(q, m, c) if core == 0 else pb_buf.at[q, m - 1, :, prompt_cols(q)]
        dst = prompt_place(q, c if core == 0 else 1 - c)
        return remote(src, dst, px_send.at[q, m - 1, core], px_recv.at[q, m - 1, core], at_x(m))

    def prompt_own(q):
        return pltpu.make_async_copy(prompt_part(q, 0, c), prompt_place(q, c), own_sem.at[q])

    def prompt_y(q, m):
        block = x_buf.at[0, q, :, :, :, prompt_cols(q)]
        return remote(block, block, py_send.at[q, m - 1], py_recv.at[q, m - 1], at_y(m))

    def prompt_start(q):
        prompt_own(q).start()
        for m in (2, 1, 3):
            send(prompt_x(q, m, 0))

    def prompt_forward(q):
        for m in (2, 1, 3):
            prompt_core(q, m).wait_recv()
            send(prompt_x(q, m, 1))

    def prompt_along_x(q):
        prompt_own(q).wait()
        prompt_core(q, 0).wait_recv()
        for m in (1, 3, 2):
            for core in (0, 1):
                prompt_x(q, m, core).wait_recv()

    def prompt_along_y(q):
        prompt_along_x(q)
        for m in (2, 1, 3):
            send(prompt_y(q, m))

    dec_block = x_buf.at[1, my_q, y, my_zh]
    for q in range(NQ):
        for m in (2, 1, 3, 0):
            send(prompt_core(q, m))
        if q == 0:
            prompt_start(0)
            for m in (4, 3, 5, 2, 6, 1, 7):
                send(remote(dec_block, dec_block, dz_send.at[m - 1], dz_recv.at[z], at_z(m)))
    prompt_forward(0)
    for q in range(DIRECT, NQ):
        prompt_start(q)
        prompt_forward(q)
    for q in range(1, DIRECT):
        prompt_start(q)
        prompt_forward(q)

    def decode_y(q):
        for zh in (0, 1):
            block = x_buf.at[1, q, y, zh]

            @pl.when(z != zh * NQ + q)
            def _():
                remote(block, block, dz_send.at[0], dz_recv.at[zh * NQ + q], at_z(1)).wait_recv()

        for m in (1, 3, 2):
            send(decode_y_copy(q, m))

    def decode_y_copy(q, m):
        block = x_buf.at[1, q, y]
        return remote(block, block, dy_send.at[q, m - 1], dy_recv.at[q, m - 1], at_y(m))

    def wait_input(k):
        if k < DIRECT:
            prompt_along_x(k)
        elif k < NQ:
            for m in (1, 3, 2):
                prompt_y(k, m).wait_recv()
        else:
            for m in (1, 3, 2):
                decode_y_copy(k - NQ, m).wait_recv()

    def dequant_gate_up(i):
        for load in loads[i]:
            load.wait()

        def tile(j, carry):
            cols = pl.ds(pl.multiple_of(j * 256, 256), 256)
            for r in range(i * part // 128, (i + 1) * part // 128):
                rows = pl.ds(r * 128, 128)
                w[rows, cols] = (w[rows, cols].astype(F32) * sc[pl.ds(r, 1), cols]).astype(BF)
            return carry

        lax.fori_loop(0, 2 * ff // 256, tile, 0)

    def dequant_down():
        for load in down_loads:
            load.wait()

        def tile(j, carry):
            rows = pl.ds(pl.multiple_of(j * 128, 128), 128)
            scales = ds[:, rows].T
            for b in range(8):
                cols = pl.ds(b * 128, 128)
                wd[rows, cols] = (wd[rows, cols].astype(F32) * scales[:, b : b + 1]).astype(BF)
            return carry

        lax.fori_loop(0, ff // 128, tile, 0)

    theirs = pl.ds(pl.multiple_of((1 - c) * HALF, HALF), HALF)
    sides = (pl.ds(0, ff), pl.ds(ff, ff))

    def exchange(k, s):
        return remote(
            p_buf.at[k, theirs, sides[s]], px_buf.at[k, :, sides[s]], ex_send.at[k, s], ex_recv.at[k, s], partner
        )

    def stage1(k):
        wait_input(k)
        rows = x_buf[k // NQ, k % NQ].reshape(ROWS, width)
        for s in (0, 1):
            p_buf[k, :, sides[s]] = jnp.dot(rows, w[:, sides[s]], preferred_element_type=F32).astype(BF)
            send(exchange(k, s))

    def pair_sum(k, at, s):
        own = pl.ds(pl.multiple_of(c * HALF + at * PIECE, PIECE), PIECE)
        got = pl.ds(pl.multiple_of(at * PIECE, PIECE), PIECE)
        return p_buf[k, own, sides[s]].astype(F32) + px_buf[k, got, sides[s]].astype(F32)

    def q_copy(k, kind, d):
        src = q_buf.at[k, kind, d]
        if kind == 0:
            return remote(src, m1_buf.at[k, d], q_send.at[k, 0, d], m1_recv.at[k, d], side[d])
        s = 1 - d if kind == 1 else d
        return remote(src, m2_buf.at[k, d, s], q_send.at[k, kind, d], m2_recv.at[k, kind - 1, d], side[d])

    def stage2(k):
        for s in (0, 1):
            exchange(k, s).wait_recv()
            q_buf[k, 0, s] = pair_sum(k, across, s).astype(BF)
            send(q_copy(k, 0, s))
        for s in (0, 1):
            q_buf[k, 1, 1 - s] = pair_sum(k, chip[1 - s], s).astype(BF)
            send(q_copy(k, 1, 1 - s))

    def stage3(k):
        for d in (0, 1):
            q_copy(k, 0, d).wait_recv()
            q_buf[k, 2, d] = (pair_sum(k, chip[d], d) + m1_buf[k, d].astype(F32)).astype(BF)
            send(q_copy(k, 2, d))

    def piece(k, core, at, cols=pl.ds(0, 1664)):
        return h_buf.at[k, pl.ds(pl.multiple_of(core * HALF + at * PIECE, PIECE), PIECE), cols]

    cut = ff // 256 * 128 + 128
    cuts = (pl.ds(0, cut), pl.ds(cut, ff - cut))

    def a_copy(k, step, d):
        block = piece(k, c, x) if step == 0 else piece(k, c, chip[1 - d], cuts[d])
        return remote(block, block, a_send.at[k, step, d], a_recv.at[k, step, d], side[d])

    def c_copy(k, i):
        block = piece(k, c, (x, chip[0], chip[1], across)[i])
        return remote(block, block, c_send.at[k, i], c_recv.at[k, i], partner)

    def stage4(k):
        for kind in (1, 2):
            for d in (0, 1):
                q_copy(k, kind, d).wait_recv()
        g, u = [
            pair_sum(k, x, s) + m2_buf[k, 0, s].astype(F32) + m2_buf[k, 1, s].astype(F32) for s in (0, 1)
        ]
        own = pl.ds(pl.multiple_of(c * HALF + x * PIECE, PIECE), PIECE)
        h_buf[k, own, :] = (g / (1.0 + jnp.exp(-g)) * u).astype(BF)
        for d in (0, 1):
            send(a_copy(k, 0, d))
        send(c_copy(k, 0))

    def stage5(k):
        for d in (0, 1):
            a_copy(k, 0, d).wait_recv()
            send(a_copy(k, 1, d))
        send(c_copy(k, 1))
        send(c_copy(k, 2))

    def stage6(k):
        for d in (0, 1):
            a_copy(k, 1, d).wait_recv()
        send(c_copy(k, 3))

    def y_copy(k, m):
        return remote(
            o_buf.at[k, lax.rem(y + m, NY)], ry_buf.at[k, m - 1], y_send.at[k, m - 1], y_recv.at[k, m - 1], at_y(m)
        )

    def stage7(k):
        for i in range(4):
            c_copy(k, i).wait_recv()
        product = jnp.dot(h_buf[k], wd[...], preferred_element_type=F32)
        o_buf[k] = product.astype(BF).reshape(NY, ROWS // NY, width)
        for m in (1, 3, 2):
            send(y_copy(k, m))

    def z_copy(k, zh):
        to = zh * NQ + k % NQ
        slot = lax.rem(to - z + 2 * NZ - 1, NZ)
        return to, remote(
            sy_buf.at[k, pl.ds(zh * GROUP, GROUP), :], rz_buf.at[k // NQ, slot],
            z_send.at[k, zh], z_recv.at[k // NQ, slot], (gx, y * NZ + to),
        )

    def stage8(k):
        for m in (1, 3, 2):
            y_copy(k, m).wait_recv()
        for j in range(0, width, 256):
            cols = pl.ds(j, 256)
            total = o_buf[k, y, :, cols].astype(F32)
            for m in range(3):
                total = total + ry_buf[k, m, :, cols].astype(F32)
            sy_buf[k, :, cols] = total.astype(BF)
        for zh in (0, 1):
            to, copy = z_copy(k, zh)

            @pl.when(to != z)
            def _():
                copy.start()

    def finish(kind):
        for m in range(NZ - 1):
            slot = rz_buf.at[kind, m]
            remote(slot, slot, z_send.at[0, 0], z_recv.at[kind, m], at_z(1)).wait_recv()
        rows = pl.ds(pl.multiple_of(my_zh * GROUP, GROUP), GROUP)
        for j in range(0, width, 256):
            cols = pl.ds(j, 256)
            total = sy_buf[kind * NQ + my_q, rows, cols].astype(F32)
            for m in range(NZ - 1):
                total = total + rz_buf[kind, m, :, cols].astype(F32)
            total = total.astype(BF)
            out[kind, :, cols] = total

    stages = (stage1, stage2, stage3, stage4, stage5, stage6, stage7, stage8)
    for i in range(DEQ):
        dequant_gate_up(i)
        if i == DEQ - 2:
            for load in down_loads:
                load.start()
    for q in range(DIRECT, NQ):
        prompt_along_y(q)
    for i, k in stage_order():
        if (i, k) == (1, 0):
            for q in range(NQ):
                decode_y(q)
        if (i, k) == (1, 1):
            dequant_down()
        stages[i](k)
    finish(0)
    finish(1)

    for copy in pending:
        copy.wait_send()
    for k in range(CHUNKS):
        for zh in (0, 1):
            to, copy = z_copy(k, zh)

            @pl.when(to != z)
            def _():
                copy.wait_send()


def split_kernel(both, prompt_out, dec_out):
    prompt_out[...] = both[0]
    dec_out[0] = both[1, 0:8]
    dec_out[1] = both[1, 8:16]


def body(prompt, dec_in, gate_codes, gate_scale, up_codes, up_scale, down_codes, down_scale):
    width, ff = gate_codes.shape
    dma = pltpu.SemaphoreType.DMA
    any_spec = pl.BlockSpec(memory_space=pl.ANY)
    vmem = pl.BlockSpec(memory_space=pltpu.VMEM)
    both = pl.pallas_call(
        kernel,
        out_shape=jax.ShapeDtypeStruct((2, GROUP, width), BF),
        in_specs=[any_spec] * 8,
        out_specs=vmem,
        scratch_shapes=[
            pltpu.VMEM((width, 2 * ff), BF),
            pltpu.VMEM((8, 2 * ff), F32),
            pltpu.VMEM((ff, width), BF),
            pltpu.VMEM((8, ff), F32),
            pltpu.VMEM((2, NQ, NY, 2, GROUP, width), BF),
            pltpu.VMEM((NQ, NX - 1, GROUP, width), BF),
            pltpu.VMEM(dec_in.shape, BF),
            pltpu.VMEM((CHUNKS, ROWS, 2 * ff), BF),
            pltpu.VMEM((CHUNKS, HALF, 2 * ff), BF),
            pltpu.VMEM((CHUNKS, 3, 2, PIECE, ff), BF),
            pltpu.VMEM((CHUNKS, 2, PIECE, ff), BF),
            pltpu.VMEM((CHUNKS, 2, 2, PIECE, ff), BF),
            pltpu.VMEM((CHUNKS, ROWS, ff), BF),
            pltpu.VMEM((CHUNKS, NY, ROWS // NY, width), BF),
            pltpu.VMEM((CHUNKS, 3, ROWS // NY, width), BF),
            pltpu.VMEM((CHUNKS, ROWS // NY, width), BF),
            pltpu.VMEM((2, NZ - 1, GROUP, width), BF),
            dma((DEQ + 1, 2)),
            dma((2,)),
            dma((1,)),
            dma((NQ,)),
            dma((NQ, NX)),
            dma((NQ, NX)),
            dma((NQ, NX - 1, 2)),
            dma((NQ, NX - 1, 2)),
            dma((NQ, NY - 1)),
            dma((NQ, NY - 1)),
            dma((NZ - 1,)),
            dma((NZ,)),
            dma((NQ, NY - 1)),
            dma((NQ, NY - 1)),
            dma((CHUNKS, 2)),
            dma((CHUNKS, 2)),
            dma((CHUNKS, 3, 2)),
            dma((CHUNKS, 2)),
            dma((CHUNKS, 2, 2)),
            dma((CHUNKS, 2, 2)),
            dma((CHUNKS, 2, 2)),
            dma((CHUNKS, 4)),
            dma((CHUNKS, 4)),
            dma((CHUNKS, 3)),
            dma((CHUNKS, 3)),
            dma((CHUNKS, 2)),
            dma((2, NZ - 1)),
        ],
        compiler_params=pltpu.CompilerParams(
            collective_id=0, has_side_effects=True, vmem_limit_bytes=60 * 1024 * 1024
        ),
        cost_estimate=pl.CostEstimate(flops=10_500_000_000, bytes_accessed=12_000_000, transcendentals=1_000_000),
        name="ffn",
    )(
        prompt.reshape(NQ, GROUP, prompt.shape[1]), dec_in, gate_codes, gate_scale, up_codes, up_scale, down_codes,
        down_scale.T,
    )
    return pl.pallas_call(
        split_kernel,
        out_shape=(
            jax.ShapeDtypeStruct((GROUP, width), BF),
            jax.ShapeDtypeStruct(dec_in.shape, BF),
        ),
        in_specs=[vmem],
        out_specs=(vmem, vmem),
        name="split",
    )(both)


def solution(mesh):
    in_specs = (
        P("gx", None),
        P(None, "gy", "gx"),
        P("gx", "gy"),
        P("gx", "gy"),
        P("gx", "gy"),
        P("gx", "gy"),
        P("gy", "gx"),
        P("gy", "gx"),
    )
    out_specs = (P("gy", "gx"), P(None, "gy", "gx"))
    return jax.shard_map(body, mesh=mesh, in_specs=in_specs, out_specs=out_specs, check_vma=False)
```
